32 devices in a mesh: tm: 16 (over z, x, core), head: 2 (over y).
Axes of the slice: x: 2, y: 2, z: 4, core: 2. Of those that a mesh axis runs over, the one named last changes fastest.
Arguments:
- frames: bfloat16 [32768, 1024], P('tm'), may hold values from -6 to 6
- conv_weight: bfloat16 [4, 1024], replicated, may hold values from -3 to 3
- w_query: bfloat16 [1024, 1024], P(None, 'head'), may hold values from -0.1875 to 0.1875
- w_key: bfloat16 [1024, 1024], P(None, 'head'), may hold values from -0.1875 to 0.1875
- w_value: bfloat16 [1024, 1024], P(None, 'head'), may hold values from -0.1875 to 0.1875
- w_gate: bfloat16 [1024, 1024], P(None, 'head'), may hold values from -0.1875 to 0.1875
- w_out: bfloat16 [1024, 1024], P('head'), may hold values from -0.1875 to 0.1875
- norm_gain: float32 [1024], P('head'), may hold values from 0.1 to 1.9
Outputs:
- layer_out: bfloat16 [32768, 1024], P('tm', 'head')
The draws below stay inside these ranges and needn't reach their ends.
All inputs are finite; a program needn't handle non-finite values.
Results may differ from the reference program's by a relative error of at most 0.014.
Values may be sent and summed in bfloat16 or wider, within the bound.
A program may use at most 64 MiB of HBM per device.

```python
import jax
import jax.numpy as jnp
from jax import lax

D = 1024
HEADS = 8
HEAD_DIM = 128
CONV = 4
BLOCK = 512
SEQ = 32768
N_HEAD = 2


def block_scale(rng, shape, shards, low, top_value):
    def one(position, shards_of):
        heights = jax.random.uniform(jax.random.fold_in(jax.random.fold_in(rng, 6), position), (shards_of,), jnp.float32, low / len(shards), top_value / len(shards))
        return jnp.repeat(jnp.exp(heights), shape[position] // shards_of).reshape((-1,) + (1,) * (len(shape) - position - 1))

    loudness = one(*shards[0])
    for cut in shards[1:]:
        loudness = loudness * one(*cut)
    return loudness


def centred(stream_key, shape, scale, bound, shards=(), held_as=jnp.bfloat16):
    values = scale * jax.random.normal(stream_key, shape, jnp.float32)
    if shards:
        values = values * block_scale(stream_key, shape, shards, -0.22, 0.18)
    return jnp.clip(values, -bound, bound).astype(held_as)


def setup_inputs(seed: int = 0) -> dict:
    streams_of = jax.random.split(jax.random.key(seed), 9)
    return {
        "frames": centred(streams_of[0], (SEQ, D), 1.0, 6.0, ((0, 16),)),
        "conv_weight": centred(streams_of[1], (CONV, D), 0.5, 3.0),
        "w_query": centred(streams_of[2], (D, D), D ** -0.5, 0.1875, ((1, 2),)),
        "w_key": centred(streams_of[3], (D, D), D ** -0.5, 0.1875, ((1, 2),)),
        "w_value": centred(streams_of[4], (D, D), D ** -0.5, 0.1875, ((1, 2),)),
        "w_gate": centred(streams_of[5], (D, D), D ** -0.5, 0.1875, ((1, 2),)),
        "w_out": centred(streams_of[6], (D, D), D ** -0.5, 0.1875, ((0, 2),)),
        "norm_gain": jnp.clip(1.0 + 0.18 * jax.random.normal(streams_of[7], (D,), jnp.float32), 0.1, 1.9),
    }


def feature_map(inputs):
    return jnp.where(inputs > 0, inputs + 1.0, jnp.exp(jnp.minimum(inputs, 0.0)))

def reference(frames, conv_weight, w_query, w_key, w_value, w_gate, w_out, norm_gain):
    padded = jnp.concatenate([jnp.zeros((CONV - 1, D), jnp.float32), frames.astype(jnp.float32)], axis=0)
    taps = conv_weight.astype(jnp.float32)
    mixed = taps[0] * padded[0:SEQ]
    for offset in range(1, CONV):
        mixed = mixed + taps[offset] * padded[offset:offset + SEQ]
    smooth = mixed.astype(jnp.bfloat16)
    queries = feature_map(jnp.dot(smooth, w_query, preferred_element_type=jnp.float32)).astype(jnp.bfloat16)
    key_feats = feature_map(jnp.dot(smooth, w_key, preferred_element_type=jnp.float32)).astype(jnp.bfloat16)
    values = jnp.dot(smooth, w_value, preferred_element_type=jnp.float32).astype(jnp.bfloat16)
    gates = jnp.dot(smooth, w_gate, preferred_element_type=jnp.float32)
    blocks = SEQ // BLOCK
    block_shape = (blocks, BLOCK, HEADS, HEAD_DIM)
    causal = jnp.tril(jnp.ones((BLOCK, BLOCK), jnp.bool_))

    def advance(kv_state, inputs):
        query_blk = inputs[0].astype(jnp.float32)
        key_blk = inputs[1].astype(jnp.float32)
        value_blk = inputs[2].astype(jnp.float32)
        scores = jnp.einsum('thd,shd->hts', query_blk, key_blk)
        scores = jnp.where(causal[None], scores, 0.0).astype(jnp.bfloat16).astype(jnp.float32)
        carried = kv_state.astype(jnp.bfloat16).astype(jnp.float32)
        result = jnp.einsum('hts,shd->thd', scores, value_blk) + jnp.einsum('thd,hde->the', query_blk, carried)
        kv_state = kv_state + jnp.einsum('thd,the->hde', key_blk, value_blk)
        return (kv_state, result)
    start_state = jnp.zeros((HEADS, HEAD_DIM, HEAD_DIM), jnp.float32)
    _, outputs = lax.scan(advance, start_state, (queries.reshape(block_shape), key_feats.reshape(block_shape), values.reshape(block_shape)))
    attended = outputs.reshape(SEQ, HEADS, HEAD_DIM)
    mean_square = lax.optimization_barrier(jnp.mean(attended * attended, axis=-1, keepdims=True))
    normed = attended * lax.rsqrt(mean_square + 1e-06) * norm_gain.reshape(HEADS, HEAD_DIM)
    normed = normed * jax.nn.silu(gates).reshape(SEQ, HEADS, HEAD_DIM)
    gated = normed.reshape(SEQ, D).astype(jnp.bfloat16)
    width = D // N_HEAD
    total = jnp.zeros((SEQ, D), jnp.float32)
    for group_index in range(N_HEAD):
        lower = group_index * width
        partial_value = jnp.dot(gated[:, lower:lower + width], w_out[lower:lower + width], preferred_element_type=jnp.float32)
        total = total + partial_value.astype(jnp.bfloat16).astype(jnp.float32)
    return total.astype(jnp.bfloat16)
```

```python
import functools

import jax
import jax.numpy as jnp
from jax import lax
from jax.experimental import pallas as pl
from jax.experimental.pallas import tpu as pltpu
from jax.sharding import PartitionSpec as P

HEAD_DIM = 128
CONV = 4
BLOCK = 512


def from_behind(array, axis, by):
    devices = lax.axis_size(axis)
    pairs = [(i, i + by) for i in range(devices) if 0 <= i + by < devices]
    return lax.ppermute(array, axis, pairs)


def feature_map(inputs):
    return jnp.where(inputs > 0, inputs + 1.0, jnp.exp(jnp.minimum(inputs, 0.0)))


def on_device_collectives(frames, conv_weight, w_query, w_key, w_value, w_gate, w_out, norm_gain):
    tok_rows = frames.shape[0]
    edge_rows = from_behind(frames[tok_rows - (CONV - 1) :], "tm", 1)
    padded = jnp.concatenate([edge_rows, frames], axis=0)
    taps = conv_weight.astype(jnp.float32)
    mixed = taps[0] * padded[0:tok_rows].astype(jnp.float32)
    for offset in range(1, CONV):
        mixed = mixed + taps[offset] * padded[offset : offset + tok_rows].astype(jnp.float32)
    smooth = mixed.astype(jnp.bfloat16)
    queries = feature_map(jnp.dot(smooth, w_query, preferred_element_type=jnp.float32)).astype(
        jnp.bfloat16
    )
    key_feats = feature_map(jnp.dot(smooth, w_key, preferred_element_type=jnp.float32)).astype(
        jnp.bfloat16
    )
    values = jnp.dot(smooth, w_value, preferred_element_type=jnp.float32).astype(jnp.bfloat16)
    gates = jnp.dot(smooth, w_gate, preferred_element_type=jnp.float32)
    heads_here = w_query.shape[1] // HEAD_DIM
    blocks = tok_rows // BLOCK
    block_shape = (blocks, BLOCK, heads_here, HEAD_DIM)
    query_blocks = queries.reshape(block_shape)
    key_blocks = key_feats.reshape(block_shape)
    value_blocks = values.reshape(block_shape)
    block_states = jnp.einsum(
        "bthd,bthe->bhde", key_blocks, value_blocks, preferred_element_type=jnp.float32
    )
    own_total = jnp.sum(block_states, axis=0)
    position = lax.axis_index("tm")
    shard_piece = lax.all_gather(own_total[None], "tm", axis=0, tiled=True)
    source_rank = jnp.arange(shard_piece.shape[0], dtype=jnp.int32)
    earlier_mask = (source_rank < position).astype(jnp.float32)
    incoming = jnp.sum(shard_piece * earlier_mask[:, None, None, None], axis=0)
    running_sums = jnp.cumsum(block_states, axis=0)
    exclusive = jnp.concatenate([jnp.zeros_like(block_states[:1]), running_sums[:-1]], axis=0)
    carried = (incoming[None] + exclusive).astype(jnp.bfloat16)
    causal = jnp.tril(jnp.ones((BLOCK, BLOCK), jnp.bool_))
    scores = jnp.einsum(
        "bthd,bshd->bhts", query_blocks, key_blocks, preferred_element_type=jnp.float32
    )
    scores = jnp.where(causal[None, None], scores, 0.0).astype(jnp.bfloat16)
    attended = jnp.einsum(
        "bhts,bshd->bthd", scores, value_blocks, preferred_element_type=jnp.float32
    )
    attended = attended + jnp.einsum(
        "bthd,bhde->bthe", query_blocks, carried, preferred_element_type=jnp.float32
    )
    attended = attended.reshape(tok_rows, heads_here, HEAD_DIM)
    mean_square = jnp.mean(attended * attended, axis=-1, keepdims=True)
    normed = attended * lax.rsqrt(mean_square + 1e-06) * norm_gain.reshape(heads_here, HEAD_DIM)
    normed = normed * jax.nn.silu(gates).reshape(tok_rows, heads_here, HEAD_DIM)
    gated = normed.reshape(tok_rows, heads_here * HEAD_DIM).astype(jnp.bfloat16)
    partial_value = jnp.dot(gated, w_out, preferred_element_type=jnp.float32)
    summed = lax.psum_scatter(
        partial_value.astype(jnp.bfloat16), "head", scatter_dimension=1, tiled=True
    )
    return summed


F32 = jnp.float32
BF16 = jnp.bfloat16
MESH = pl.DeviceIdType.MESH
N_COPIES = 29


def fused_kernel(
    n_tm, frames, conv, wq, wk, wv, wg, wo, gain, out,
    smooth, qs, ks, vs, gs, wx, wox, gainx, halo, ext, state, carried,
    total, pair, before, incoming,
    s_tot, r_tot, s_pair, r_pair, s_grp, r_grp, s_bef, r_bef, s_inc, r_inc,
    send_sem, recv_sem,
):
    t = lax.axis_index("tm")
    h = lax.axis_index("head")
    rows = frames.shape[0]
    half = wq.shape[1]
    heads = half // HEAD_DIM
    blocks = rows // BLOCK
    depth = wq.shape[0]
    quarter = depth // 4
    quarter_o = half // 4
    n_z = n_tm // 4
    z = lax.div(t, 4)
    r = lax.rem(t, 4)
    x = lax.div(r, 2)
    c = lax.rem(t, 2)
    other_core = {"tm": t + 1 - 2 * c}
    other_x = {"tm": t + 2 - 4 * x}
    other_y = {"head": 1 - h}
    after = {"tm": lax.rem(t + 1, n_tm)}
    ahead = {"tm": lax.rem(t + n_tm - 1, n_tm)}
    zs = [{"tm": lax.rem(z + d, n_z) * 4 + r} for d in range(1, n_z)]
    r_x = r + 2 - 4 * x

    barrier = pltpu.get_barrier_semaphore()
    peers = [other_core, other_x, other_y, after, ahead] + zs
    for peer in peers:
        pl.semaphore_signal(barrier, inc=1, device_id=peer, device_id_type=MESH)
    pl.semaphore_wait(barrier, len(peers))

    copies = []

    def send(src, dst, device):
        n = len(copies)
        copy = pltpu.make_async_remote_copy(
            src_ref=src, dst_ref=dst, send_sem=send_sem.at[n], recv_sem=recv_sem.at[n],
            device_id=device, device_id_type=MESH,
        )
        copy.start()
        copies.append(copy)
        return copy

    def piece(m, which):
        if m == 4:
            return wox.at[pl.ds(pl.multiple_of(which * quarter_o, quarter_o), quarter_o), :]
        return wx.at[m, pl.ds(pl.multiple_of(which * quarter, quarter), quarter), :]

    edge = send(frames.at[pl.ds(rows - 16, 16), :], halo, after)
    from_y, from_x, from_core = {}, {}, {}
    for m, weight in enumerate((wk, wv, wq, wg)):
        mine = weight.at[pl.ds(pl.multiple_of(r * quarter, quarter), quarter), :]
        from_y[m] = send(mine, piece(m, r), other_y)
    mine = wo.at[
        pl.ds(pl.multiple_of(r * quarter_o, quarter_o), quarter_o),
        pl.ds(pl.multiple_of((1 - h) * half, half), half),
    ]
    from_y[4] = send(mine, piece(4, r), other_y)
    gain_copy = send(gain, gainx, other_y)

    def relay_y(m):
        from_y[m].wait_recv()
        from_x[m] = send(piece(m, r), piece(m, r), other_x)
        from_core[m] = [send(piece(m, r), piece(m, r), other_core)]

    def relay_x(m):
        from_x[m].wait_recv()
        from_core[m].append(send(piece(m, r_x), piece(m, r_x), other_core))

    def ready(m):
        for copy in from_core[m]:
            copy.wait_recv()

    chunk = BLOCK // 2
    taps = conv[...].astype(F32)

    def mix(first):
        ext[16 : 16 + chunk, :] = frames[pl.ds(first, chunk), :].astype(F32)
        mixed = taps[0:1] * ext[13 : 13 + chunk, :]
        for j in range(1, CONV):
            mixed = mixed + taps[j : j + 1] * ext[13 + j : 13 + j + chunk, :]
        smooth[pl.ds(first, chunk), :] = mixed.astype(BF16)

    def mix_chunk(i, _):
        first = pl.multiple_of(i * chunk, chunk)
        ext[0:16, :] = frames[pl.ds(pl.multiple_of(first - 16, 16), 16), :].astype(F32)
        mix(first)
        return 0

    lax.fori_loop(1, rows // chunk, mix_chunk, 0)
    edge.wait_recv()
    ext[0:16, :] = halo[...].astype(F32) * jnp.minimum(t, 1).astype(F32)
    mix(0)

    def project(weight, into, which, function):
        def step(i, _):
            at = pl.ds(pl.multiple_of(i * BLOCK, BLOCK), BLOCK)
            product = jnp.dot(smooth[at, :], weight[...], preferred_element_type=F32)
            into[which, at, :] = function(product).astype(BF16)
            return 0

        lax.fori_loop(0, blocks, step, 0)

    def silu_by(gain_ref):
        def function(v):
            return (0.5 * v) * (1.0 + jnp.tanh(0.5 * v)) * gain_ref[...]

        return function

    def same(v):
        return v

    def states(which):
        def step(b, _):
            at = pl.ds(pl.multiple_of(b * BLOCK, BLOCK), BLOCK)
            for j in range(heads):
                cols = slice(j * HEAD_DIM, (j + 1) * HEAD_DIM)
                state[which, b, cols, :] = lax.dot_general(
                    ks[which, at, cols], vs[which, at, cols],
                    (((0,), (0,)), ((), ())), preferred_element_type=F32,
                )
            return 0

        lax.fori_loop(0, blocks, step, 0)

    def carry(which, start_ref):
        running = start_ref[...].astype(F32)
        for b in range(blocks):
            carried[which, b] = running.astype(BF16)
            if b + 1 < blocks:
                running = running + state[which, b]

    row_id = lax.broadcasted_iota(jnp.int32, (chunk, chunk), 0)
    col_id = lax.broadcasted_iota(jnp.int32, (chunk, chunk), 1)
    causal = col_id <= row_id
    nt = (((1,), (1,)), ((), ()))

    def attend(which):
        def step(b, _):
            low = pl.ds(pl.multiple_of(b * BLOCK, BLOCK), chunk)
            high = pl.ds(pl.multiple_of(b * BLOCK + chunk, chunk), chunk)
            for j in range(heads):
                cols = slice(j * HEAD_DIM, (j + 1) * HEAD_DIM)
                q0, q1 = qs[which, low, cols], qs[which, high, cols]
                k0, k1 = ks[which, low, cols], ks[which, high, cols]
                v0, v1 = vs[which, low, cols], vs[which, high, cols]
                start = carried[which, b, cols, :]
                s00 = lax.dot_general(q0, k0, nt, preferred_element_type=F32)
                s10 = lax.dot_general(q1, k0, nt, preferred_element_type=F32)
                s11 = lax.dot_general(q1, k1, nt, preferred_element_type=F32)
                s00 = jnp.where(causal, s00, 0.0).astype(BF16)
                s11 = jnp.where(causal, s11, 0.0).astype(BF16)
                a0 = jnp.dot(s00, v0, preferred_element_type=F32)
                a0 = a0 + jnp.dot(q0, start, preferred_element_type=F32)
                a1 = jnp.dot(s10.astype(BF16), v0, preferred_element_type=F32)
                a1 = a1 + jnp.dot(s11, v1, preferred_element_type=F32)
                a1 = a1 + jnp.dot(q1, start, preferred_element_type=F32)
                for at, a in ((low, a0), (high, a1)):
                    scale = lax.rsqrt(jnp.mean(a * a, axis=-1, keepdims=True) + 1e-06)
                    gated = a * scale * gs[which, at, cols].astype(F32)
                    qs[which, at, cols] = gated.astype(BF16)
            return 0

        lax.fori_loop(0, blocks, step, 0)

    here = pl.ds(pl.multiple_of(c * (half // 2), half // 2), half // 2)
    there = pl.ds(pl.multiple_of((1 - c) * (half // 2), half // 2), half // 2)

    project(wk, ks, 0, feature_map)
    relay_y(0)
    project(wv, vs, 0, same)
    states(0)
    sums = state[0, 0]
    for b in range(1, blocks):
        sums = sums + state[0, b]
    total[...] = sums
    s_tot[...] = sums.astype(BF16)
    tot_copy = send(s_tot, r_tot, other_core)
    project(wq, qs, 0, feature_map)
    relay_y(1)
    relay_x(0)
    tot_copy.wait_recv()
    pair[...] = total[...] + r_tot[...].astype(F32)
    s_pair[...] = pair[here, :].astype(BF16)
    pair_copy = send(s_pair, r_pair, other_x)
    project(wg, gs, 0, silu_by(gain))
    relay_y(2)
    relay_x(1)
    pair_copy.wait_recv()
    s_grp[...] = (pair[here, :] + r_pair[...].astype(F32)).astype(BF16)
    grp_copies = [send(s_grp, r_grp.at[d], device) for d, device in enumerate(zs)]
    ready(0)
    project(wx.at[0], ks, 1, feature_map)
    for copy in grp_copies:
        copy.wait_recv()
    sums = r_pair[...].astype(F32) * x.astype(F32)
    for d in range(1, n_z):
        earlier = jnp.where(z >= d, 1.0, 0.0)
        sums = sums + r_grp[d - 1].astype(F32) * earlier
    before[...] = sums
    s_bef[...] = sums.astype(BF16)
    bef_copy = send(s_bef, r_bef, other_core)
    relay_y(3)
    relay_x(2)
    ready(1)
    project(wx.at[1], vs, 1, same)
    states(1)
    bef_copy.wait_recv()
    incoming[here, :] = before[...]
    incoming[there, :] = r_bef[...].astype(F32)
    incoming[...] = incoming[...] + r_tot[...].astype(F32) * c.astype(F32)
    s_inc[...] = incoming[...].astype(BF16)
    inc_copy = send(s_inc, r_inc, other_y)
    relay_y(4)
    relay_x(3)
    carry(0, incoming)
    attend(0)
    relay_x(4)
    ready(2)
    project(wx.at[2], qs, 1, feature_map)
    gain_copy.wait_recv()
    ready(3)
    project(wx.at[3], gs, 1, silu_by(gainx))
    inc_copy.wait_recv()
    carry(1, r_inc)
    attend(1)
    ready(4)

    def project_out(i, _):
        at = pl.ds(pl.multiple_of(i * BLOCK, BLOCK), BLOCK)
        w_here = wo[:, pl.ds(pl.multiple_of(h * half, half), half)]
        first = jnp.dot(qs[0, at, :], w_here, preferred_element_type=F32)
        second = jnp.dot(qs[1, at, :], wox[...], preferred_element_type=F32)
        out[at, :] = (first + second).astype(BF16)
        return 0

    lax.fori_loop(0, blocks, project_out, 0)
    for copy in copies:
        copy.wait_send()


def on_device_fused(n_tm, frames, conv_weight, w_query, w_key, w_value, w_gate, w_out, norm_gain):
    rows, depth = frames.shape
    half = w_query.shape[1]
    blocks = rows // BLOCK
    chunk = BLOCK // 2
    state_rows = half
    vmem = pl.BlockSpec(memory_space=pltpu.VMEM)
    act = pltpu.VMEM((2, rows, half), BF16)
    whole = (state_rows, HEAD_DIM)
    split = (state_rows // 2, HEAD_DIM)
    return pl.pallas_call(
        functools.partial(fused_kernel, n_tm),
        out_shape=jax.ShapeDtypeStruct((rows, half), BF16),
        in_specs=[vmem] * 8,
        out_specs=vmem,
        scratch_shapes=[
            pltpu.VMEM((rows, depth), BF16),
            act, act, act, act,
            pltpu.VMEM((4, depth, half), BF16),
            pltpu.VMEM((half, half), BF16),
            pltpu.VMEM((1, half), F32),
            pltpu.VMEM((16, depth), BF16),
            pltpu.VMEM((16 + chunk, depth), F32),
            pltpu.VMEM((2, blocks) + whole, F32),
            pltpu.VMEM((2, blocks) + whole, BF16),
            pltpu.VMEM(whole, F32),
            pltpu.VMEM(whole, F32),
            pltpu.VMEM(split, F32),
            pltpu.VMEM(whole, F32),
            pltpu.VMEM(whole, BF16), pltpu.VMEM(whole, BF16),
            pltpu.VMEM(split, BF16), pltpu.VMEM(split, BF16),
            pltpu.VMEM(split, BF16), pltpu.VMEM((n_tm // 4 - 1,) + split, BF16),
            pltpu.VMEM(split, BF16), pltpu.VMEM(split, BF16),
            pltpu.VMEM(whole, BF16), pltpu.VMEM(whole, BF16),
            pltpu.SemaphoreType.DMA((N_COPIES,)),
            pltpu.SemaphoreType.DMA((N_COPIES,)),
        ],
        compiler_params=pltpu.CompilerParams(
            collective_id=0, has_side_effects=True, vmem_limit_bytes=60 * 2**20
        ),
    )(frames, conv_weight, w_query, w_key, w_value, w_gate, w_out, norm_gain.reshape(1, half))


def solution(mesh):
    placed = (
        P("tm", None),
        P(),
        P(None, "head"),
        P(None, "head"),
        P(None, "head"),
        P(None, "head"),
        P("head", None),
        P("head"),
    )
    n_tm = mesh.shape["tm"]
    if mesh.shape["head"] == 2 and n_tm == 16:
        on_device = functools.partial(on_device_fused, n_tm)
    else:
        on_device = on_device_collectives
    return jax.shard_map(
        on_device, mesh=mesh, in_specs=placed, out_specs=P("tm", "head"), check_vma=False
    )
```

```python
import functools

import jax
import jax.numpy as jnp
from jax import lax
from jax.experimental import pallas as pl
from jax.experimental.pallas import tpu as pltpu
from jax.sharding import PartitionSpec as P

HEAD_DIM = 128
CONV = 4
BLOCK = 512


def from_behind(array, axis, by):
    devices = lax.axis_size(axis)
    pairs = [(i, i + by) for i in range(devices) if 0 <= i + by < devices]
    return lax.ppermute(array, axis, pairs)


def feature_map(inputs):
    return jnp.where(inputs > 0, inputs + 1.0, jnp.exp(jnp.minimum(inputs, 0.0)))


def on_device_collectives(frames, conv_weight, w_query, w_key, w_value, w_gate, w_out, norm_gain):
    tok_rows = frames.shape[0]
    edge_rows = from_behind(frames[tok_rows - (CONV - 1) :], "tm", 1)
    padded = jnp.concatenate([edge_rows, frames], axis=0)
    taps = conv_weight.astype(jnp.float32)
    mixed = taps[0] * padded[0:tok_rows].astype(jnp.float32)
    for offset in range(1, CONV):
        mixed = mixed + taps[offset] * padded[offset : offset + tok_rows].astype(jnp.float32)
    smooth = mixed.astype(jnp.bfloat16)
    queries = feature_map(jnp.dot(smooth, w_query, preferred_element_type=jnp.float32)).astype(
        jnp.bfloat16
    )
    key_feats = feature_map(jnp.dot(smooth, w_key, preferred_element_type=jnp.float32)).astype(
        jnp.bfloat16
    )
    values = jnp.dot(smooth, w_value, preferred_element_type=jnp.float32).astype(jnp.bfloat16)
    gates = jnp.dot(smooth, w_gate, preferred_element_type=jnp.float32)
    heads_here = w_query.shape[1] // HEAD_DIM
    blocks = tok_rows // BLOCK
    block_shape = (blocks, BLOCK, heads_here, HEAD_DIM)
    query_blocks = queries.reshape(block_shape)
    key_blocks = key_feats.reshape(block_shape)
    value_blocks = values.reshape(block_shape)
    block_states = jnp.einsum(
        "bthd,bthe->bhde", key_blocks, value_blocks, preferred_element_type=jnp.float32
    )
    own_total = jnp.sum(block_states, axis=0)
    position = lax.axis_index("tm")
    shard_piece = lax.all_gather(own_total[None], "tm", axis=0, tiled=True)
    source_rank = jnp.arange(shard_piece.shape[0], dtype=jnp.int32)
    earlier_mask = (source_rank < position).astype(jnp.float32)
    incoming = jnp.sum(shard_piece * earlier_mask[:, None, None, None], axis=0)
    running_sums = jnp.cumsum(block_states, axis=0)
    exclusive = jnp.concatenate([jnp.zeros_like(block_states[:1]), running_sums[:-1]], axis=0)
    carried = (incoming[None] + exclusive).astype(jnp.bfloat16)
    causal = jnp.tril(jnp.ones((BLOCK, BLOCK), jnp.bool_))
    scores = jnp.einsum(
        "bthd,bshd->bhts", query_blocks, key_blocks, preferred_element_type=jnp.float32
    )
    scores = jnp.where(causal[None, None], scores, 0.0).astype(jnp.bfloat16)
    attended = jnp.einsum(
        "bhts,bshd->bthd", scores, value_blocks, preferred_element_type=jnp.float32
    )
    attended = attended + jnp.einsum(
        "bthd,bhde->bthe", query_blocks, carried, preferred_element_type=jnp.float32
    )
    attended = attended.reshape(tok_rows, heads_here, HEAD_DIM)
    mean_square = jnp.mean(attended * attended, axis=-1, keepdims=True)
    normed = attended * lax.rsqrt(mean_square + 1e-06) * norm_gain.reshape(heads_here, HEAD_DIM)
    normed = normed * jax.nn.silu(gates).reshape(tok_rows, heads_here, HEAD_DIM)
    gated = normed.reshape(tok_rows, heads_here * HEAD_DIM).astype(jnp.bfloat16)
    partial_value = jnp.dot(gated, w_out, preferred_element_type=jnp.float32)
    summed = lax.psum_scatter(
        partial_value.astype(jnp.bfloat16), "head", scatter_dimension=1, tiled=True
    )
    return summed


F32 = jnp.float32
BF16 = jnp.bfloat16
MESH = pl.DeviceIdType.MESH
N_COPIES = 29


def fused_kernel(
    n_tm, frames_hbm, conv, wq, wk, wv, wg, wo, gain, out_hbm,
    frames, own, wo_own, out,
    smooth, qs, ks, vs, gs, wx, wox, gainx, halo, ext_a, ext_b, state, carried,
    total, pair, before, incoming,
    s_tot, r_tot, s_pair, r_pair, s_grp, r_grp, s_bef, r_bef, s_inc, r_inc,
    send_sem, recv_sem, load_sem, store_sem,
):
    t = lax.axis_index("tm")
    h = lax.axis_index("head")
    rows = frames.shape[0]
    half = wq.shape[1]
    heads = half // HEAD_DIM
    blocks = rows // BLOCK
    depth = wq.shape[0]
    quarter = depth // 4
    quarter_o = half // 4
    n_z = n_tm // 4
    z = lax.div(t, 4)
    r = lax.rem(t, 4)
    x = lax.div(r, 2)
    c = lax.rem(t, 2)
    other_core = {"tm": t + 1 - 2 * c}
    other_x = {"tm": t + 2 - 4 * x}
    other_y = {"head": 1 - h}
    after = {"tm": lax.rem(t + 1, n_tm)}
    ahead = {"tm": lax.rem(t + n_tm - 1, n_tm)}
    zs = [{"tm": lax.rem(z + d, n_z) * 4 + r} for d in range(1, n_z)]
    r_x = r + 2 - 4 * x

    loads = {}

    def load(name, src, dst):
        n = len(loads)
        loads[name] = pltpu.make_async_copy(src, dst, load_sem.at[n])
        loads[name].start()

    for b in range(blocks):
        at = pl.ds(b * BLOCK, BLOCK)
        load(b, frames_hbm.at[at, :], frames.at[at, :])
    for m, weight in enumerate((wk, wv, wq, wg)):
        load(("own", m), weight, own.at[m])
    load("out", wo.at[:, pl.ds(pl.multiple_of(h * half, half), half)], wo_own)

    barrier = pltpu.get_barrier_semaphore()
    peers = [other_core, other_x, other_y, after, ahead] + zs
    for peer in peers:
        pl.semaphore_signal(barrier, inc=1, device_id=peer, device_id_type=MESH)
    pl.semaphore_wait(barrier, len(peers))

    copies = []

    def send(src, dst, device):
        n = len(copies)
        copy = pltpu.make_async_remote_copy(
            src_ref=src, dst_ref=dst, send_sem=send_sem.at[n], recv_sem=recv_sem.at[n],
            device_id=device, device_id_type=MESH,
        )
        copy.start()
        copies.append(copy)
        return copy

    def piece(m, which):
        if m == 4:
            return wox.at[pl.ds(pl.multiple_of(which * quarter_o, quarter_o), quarter_o), :]
        return wx.at[m, pl.ds(pl.multiple_of(which * quarter, quarter), quarter), :]

    edge = send(frames_hbm.at[pl.ds(rows - 16, 16), :], halo, after)
    from_y, from_x, from_core = {}, {}, {}
    for m, weight in enumerate((wk, wv, wq, wg)):
        mine = weight.at[pl.ds(pl.multiple_of(r * quarter, quarter), quarter), :]
        from_y[m] = send(mine, piece(m, r), other_y)
    mine = wo.at[
        pl.ds(pl.multiple_of(r * quarter_o, quarter_o), quarter_o),
        pl.ds(pl.multiple_of((1 - h) * half, half), half),
    ]
    from_y[4] = send(mine, piece(4, r), other_y)
    gain_copy = send(gain, gainx, other_y)

    def relay_y(m):
        from_y[m].wait_recv()
        from_x[m] = send(piece(m, r), piece(m, r), other_x)
        from_core[m] = [send(piece(m, r), piece(m, r), other_core)]

    def relay_x(m):
        from_x[m].wait_recv()
        from_core[m].append(send(piece(m, r_x), piece(m, r_x), other_core))

    def ready(m):
        for copy in from_core[m]:
            copy.wait_recv()

    chunk = BLOCK // 2
    taps = conv[...].astype(F32)

    def mix(b):
        for part, ext in ((0, ext_a), (1, ext_b)):
            first = b * BLOCK + part * chunk
            if first == 0:
                ext[0:16, :] = halo[...].astype(F32) * jnp.minimum(t, 1).astype(F32)
            else:
                ext[0:16, :] = frames[first - 16 : first, :].astype(F32)
            ext[16 : 16 + chunk, :] = frames[first : first + chunk, :].astype(F32)
            mixed = taps[0:1] * ext[13 : 13 + chunk, :]
            for j in range(1, CONV):
                mixed = mixed + taps[j : j + 1] * ext[13 + j : 13 + j + chunk, :]
            smooth[first : first + chunk, :] = mixed.astype(BF16)

    wide = 2 * HEAD_DIM

    def project_block(at, jobs):
        for weight, into, which, function in jobs:
            for first in range(0, half, wide):
                cols = slice(first, first + wide)
                product = jnp.dot(smooth[at, :], weight[:, cols], preferred_element_type=F32)
                into[which, at, cols] = function(product, cols).astype(BF16)

    def project(jobs):
        def step(i, _):
            for u in range(2):
                project_block(pl.ds(pl.multiple_of((2 * i + u) * BLOCK, BLOCK), BLOCK), jobs)
            return 0

        lax.fori_loop(0, blocks // 2, step, 0)

    def features(v, cols):
        return feature_map(v)

    def silu_by(gain_ref):
        def function(v, cols):
            return (0.5 * v) * (1.0 + jnp.tanh(0.5 * v)) * gain_ref[:, cols]

        return function

    def same(v, cols):
        return v

    def states(which):
        def step(b, _):
            at = pl.ds(pl.multiple_of(b * BLOCK, BLOCK), BLOCK)
            for first in range(0, half, wide):
                cols = slice(first, first + wide)
                both = lax.dot_general(
                    ks[which, at, cols], vs[which, at, cols],
                    (((0,), (0,)), ((), ())), preferred_element_type=F32,
                )
                for j in range(0, wide, HEAD_DIM):
                    state[which, b, first + j : first + j + HEAD_DIM, :] = both[
                        j : j + HEAD_DIM, j : j + HEAD_DIM
                    ]
            return 0

        lax.fori_loop(0, blocks, step, 0)

    def carry(which, start_ref):
        running = start_ref[...].astype(F32)
        for b in range(blocks):
            carried[which, b] = running.astype(BF16)
            if b + 1 < blocks:
                running = running + state[which, b]

    row_id = lax.broadcasted_iota(jnp.int32, (chunk, chunk), 0)
    col_id = lax.broadcasted_iota(jnp.int32, (chunk, chunk), 1)
    causal = col_id <= row_id
    nt = (((1,), (1,)), ((), ()))

    def attend(which):
        def step(b, _):
            low = pl.ds(pl.multiple_of(b * BLOCK, BLOCK), chunk)
            high = pl.ds(pl.multiple_of(b * BLOCK + chunk, chunk), chunk)
            for j in range(heads):
                cols = slice(j * HEAD_DIM, (j + 1) * HEAD_DIM)
                q0, q1 = qs[which, low, cols], qs[which, high, cols]
                k0, k1 = ks[which, low, cols], ks[which, high, cols]
                v0, v1 = vs[which, low, cols], vs[which, high, cols]
                start = carried[which, b, cols, :]
                s00 = lax.dot_general(q0, k0, nt, preferred_element_type=F32)
                s10 = lax.dot_general(q1, k0, nt, preferred_element_type=F32)
                s11 = lax.dot_general(q1, k1, nt, preferred_element_type=F32)
                s00 = jnp.where(causal, s00, 0.0).astype(BF16)
                s11 = jnp.where(causal, s11, 0.0).astype(BF16)
                a0 = jnp.dot(
                    jnp.concatenate([s00, q0], axis=1),
                    jnp.concatenate([v0, start], axis=0), preferred_element_type=F32,
                )
                a1 = jnp.dot(
                    jnp.concatenate([s10.astype(BF16), s11, q1], axis=1),
                    jnp.concatenate([v0, v1, start], axis=0), preferred_element_type=F32,
                )
                for at, a in ((low, a0), (high, a1)):
                    scale = lax.rsqrt(jnp.mean(a * a, axis=-1, keepdims=True) + 1e-06)
                    gated = a * scale * gs[which, at, cols].astype(F32)
                    qs[which, at, cols] = gated.astype(BF16)
            return 0

        lax.fori_loop(0, blocks, step, 0)

    here = pl.ds(pl.multiple_of(c * (half // 2), half // 2), half // 2)
    there = pl.ds(pl.multiple_of((1 - c) * (half // 2), half // 2), half // 2)

    own_kv = [(own.at[0], ks, 0, features), (own.at[1], vs, 0, same)]

    def first_block(b):
        project_block(pl.ds(b * BLOCK, BLOCK), own_kv)

    loads[0].wait()
    for b in range(1, blocks):
        loads[b].wait()
        if b == 2:
            loads["own", 0].wait()
            loads["own", 1].wait()
        mix(b)
        if b > 1:
            first_block(b - 1)
    edge.wait_recv()
    relay_y(0)
    mix(0)
    first_block(blocks - 1)
    first_block(0)
    states(0)
    sums = state[0, 0]
    for b in range(1, blocks):
        sums = sums + state[0, b]
    total[...] = sums
    s_tot[...] = sums.astype(BF16)
    tot_copy = send(s_tot, r_tot, other_core)
    relay_y(1)
    relay_x(0)
    loads["own", 2].wait()
    project([(own.at[2], qs, 0, features)])
    tot_copy.wait_recv()
    pair[...] = total[...] + r_tot[...].astype(F32)
    s_pair[...] = pair[here, :].astype(BF16)
    pair_copy = send(s_pair, r_pair, other_x)
    loads["own", 3].wait()
    project([(own.at[3], gs, 0, silu_by(gain))])
    relay_y(2)
    relay_x(1)
    pair_copy.wait_recv()
    s_grp[...] = (pair[here, :] + r_pair[...].astype(F32)).astype(BF16)
    grp_copies = [send(s_grp, r_grp.at[d], device) for d, device in enumerate(zs)]
    ready(0)
    project([(wx.at[0], ks, 1, features)])
    for copy in grp_copies:
        copy.wait_recv()
    sums = r_pair[...].astype(F32) * x.astype(F32)
    for d in range(1, n_z):
        earlier = jnp.where(z >= d, 1.0, 0.0)
        sums = sums + r_grp[d - 1].astype(F32) * earlier
    before[...] = sums
    s_bef[...] = sums.astype(BF16)
    bef_copy = send(s_bef, r_bef, other_core)
    relay_y(3)
    relay_x(2)
    ready(1)
    project([(wx.at[1], vs, 1, same)])
    states(1)
    bef_copy.wait_recv()
    incoming[here, :] = before[...]
    incoming[there, :] = r_bef[...].astype(F32)
    incoming[...] = incoming[...] + r_tot[...].astype(F32) * c.astype(F32)
    s_inc[...] = incoming[...].astype(BF16)
    inc_copy = send(s_inc, r_inc, other_y)
    relay_y(4)
    relay_x(3)
    carry(0, incoming)
    attend(0)
    relay_x(4)
    ready(2)
    ready(3)
    gain_copy.wait_recv()
    project([(wx.at[2], qs, 1, features), (wx.at[3], gs, 1, silu_by(gainx))])
    inc_copy.wait_recv()
    carry(1, r_inc)
    attend(1)
    ready(4)

    loads["out"].wait()
    stores = []
    for b in range(blocks):
        at = pl.ds(b * BLOCK, BLOCK)
        for first in range(0, half, wide):
            cols = slice(first, first + wide)
            here_part = jnp.dot(qs[0, at, :], wo_own[:, cols], preferred_element_type=F32)
            there_part = jnp.dot(qs[1, at, :], wox[:, cols], preferred_element_type=F32)
            out[at, cols] = (here_part + there_part).astype(BF16)
        store = pltpu.make_async_copy(out.at[at, :], out_hbm.at[at, :], store_sem.at[b])
        store.start()
        stores.append(store)
    for store in stores:
        store.wait()
    for copy in copies:
        copy.wait_send()


def on_device_fused(n_tm, frames, conv_weight, w_query, w_key, w_value, w_gate, w_out, norm_gain):
    rows, depth = frames.shape
    half = w_query.shape[1]
    blocks = rows // BLOCK
    chunk = BLOCK // 2
    state_rows = half
    vmem = pl.BlockSpec(memory_space=pltpu.VMEM)
    hbm = pl.BlockSpec(memory_space=pl.ANY)
    act = pltpu.VMEM((2, rows, half), BF16)
    whole = (state_rows, HEAD_DIM)
    split = (state_rows // 2, HEAD_DIM)
    return pl.pallas_call(
        functools.partial(fused_kernel, n_tm),
        out_shape=jax.ShapeDtypeStruct((rows, half), BF16),
        in_specs=[hbm, vmem] + [hbm] * 5 + [vmem],
        out_specs=hbm,
        scratch_shapes=[
            pltpu.VMEM((rows, depth), BF16),
            pltpu.VMEM((4, depth, half), BF16),
            pltpu.VMEM((half, half), BF16),
            pltpu.VMEM((rows, half), BF16),
            pltpu.VMEM((rows, depth), BF16),
            act, act, act, act,
            pltpu.VMEM((4, depth, half), BF16),
            pltpu.VMEM((half, half), BF16),
            pltpu.VMEM((1, half), F32),
            pltpu.VMEM((16, depth), BF16),
            pltpu.VMEM((16 + chunk, depth), F32),
            pltpu.VMEM((16 + chunk, depth), F32),
            pltpu.VMEM((2, blocks) + whole, F32),
            pltpu.VMEM((2, blocks) + whole, BF16),
            pltpu.VMEM(whole, F32),
            pltpu.VMEM(whole, F32),
            pltpu.VMEM(split, F32),
            pltpu.VMEM(whole, F32),
            pltpu.VMEM(whole, BF16), pltpu.VMEM(whole, BF16),
            pltpu.VMEM(split, BF16), pltpu.VMEM(split, BF16),
            pltpu.VMEM(split, BF16), pltpu.VMEM((n_tm // 4 - 1,) + split, BF16),
            pltpu.VMEM(split, BF16), pltpu.VMEM(split, BF16),
            pltpu.VMEM(whole, BF16), pltpu.VMEM(whole, BF16),
            pltpu.SemaphoreType.DMA((N_COPIES,)),
            pltpu.SemaphoreType.DMA((N_COPIES,)),
            pltpu.SemaphoreType.DMA((blocks + 5,)),
            pltpu.SemaphoreType.DMA((blocks,)),
        ],
        compiler_params=pltpu.CompilerParams(
            collective_id=0, has_side_effects=True, vmem_limit_bytes=60 * 2**20
        ),
    )(frames, conv_weight, w_query, w_key, w_value, w_gate, w_out, norm_gain.reshape(1, half))


def solution(mesh):
    placed = (
        P("tm", None),
        P(),
        P(None, "head"),
        P(None, "head"),
        P(None, "head"),
        P(None, "head"),
        P("head", None),
        P("head"),
    )
    n_tm = mesh.shape["tm"]
    if mesh.shape["head"] == 2 and n_tm == 16:
        on_device = functools.partial(on_device_fused, n_tm)
    else:
        on_device = on_device_collectives
    return jax.shard_map(
        on_device, mesh=mesh, in_specs=placed, out_specs=P("tm", "head"), check_vma=False
    )
```

```python
import functools

import jax
import jax.numpy as jnp
from jax import lax
from jax.experimental import pallas as pl
from jax.experimental.pallas import tpu as pltpu
from jax.sharding import PartitionSpec as P

HEAD_DIM = 128
CONV = 4
BLOCK = 512


def from_behind(array, axis, by):
    devices = lax.axis_size(axis)
    pairs = [(i, i + by) for i in range(devices) if 0 <= i + by < devices]
    return lax.ppermute(array, axis, pairs)


def feature_map(inputs):
    return jnp.where(inputs > 0, inputs + 1.0, jnp.exp(jnp.minimum(inputs, 0.0)))


def on_device_collectives(frames, conv_weight, w_query, w_key, w_value, w_gate, w_out, norm_gain):
    tok_rows = frames.shape[0]
    edge_rows = from_behind(frames[tok_rows - (CONV - 1) :], "tm", 1)
    padded = jnp.concatenate([edge_rows, frames], axis=0)
    taps = conv_weight.astype(jnp.float32)
    mixed = taps[0] * padded[0:tok_rows].astype(jnp.float32)
    for offset in range(1, CONV):
        mixed = mixed + taps[offset] * padded[offset : offset + tok_rows].astype(jnp.float32)
    smooth = mixed.astype(jnp.bfloat16)
    queries = feature_map(jnp.dot(smooth, w_query, preferred_element_type=jnp.float32)).astype(
        jnp.bfloat16
    )
    key_feats = feature_map(jnp.dot(smooth, w_key, preferred_element_type=jnp.float32)).astype(
        jnp.bfloat16
    )
    values = jnp.dot(smooth, w_value, preferred_element_type=jnp.float32).astype(jnp.bfloat16)
    gates = jnp.dot(smooth, w_gate, preferred_element_type=jnp.float32)
    heads_here = w_query.shape[1] // HEAD_DIM
    blocks = tok_rows // BLOCK
    block_shape = (blocks, BLOCK, heads_here, HEAD_DIM)
    query_blocks = queries.reshape(block_shape)
    key_blocks = key_feats.reshape(block_shape)
    value_blocks = values.reshape(block_shape)
    block_states = jnp.einsum(
        "bthd,bthe->bhde", key_blocks, value_blocks, preferred_element_type=jnp.float32
    )
    own_total = jnp.sum(block_states, axis=0)
    position = lax.axis_index("tm")
    shard_piece = lax.all_gather(own_total[None], "tm", axis=0, tiled=True)
    source_rank = jnp.arange(shard_piece.shape[0], dtype=jnp.int32)
    earlier_mask = (source_rank < position).astype(jnp.float32)
    incoming = jnp.sum(shard_piece * earlier_mask[:, None, None, None], axis=0)
    running_sums = jnp.cumsum(block_states, axis=0)
    exclusive = jnp.concatenate([jnp.zeros_like(block_states[:1]), running_sums[:-1]], axis=0)
    carried = (incoming[None] + exclusive).astype(jnp.bfloat16)
    causal = jnp.tril(jnp.ones((BLOCK, BLOCK), jnp.bool_))
    scores = jnp.einsum(
        "bthd,bshd->bhts", query_blocks, key_blocks, preferred_element_type=jnp.float32
    )
    scores = jnp.where(causal[None, None], scores, 0.0).astype(jnp.bfloat16)
    attended = jnp.einsum(
        "bhts,bshd->bthd", scores, value_blocks, preferred_element_type=jnp.float32
    )
    attended = attended + jnp.einsum(
        "bthd,bhde->bthe", query_blocks, carried, preferred_element_type=jnp.float32
    )
    attended = attended.reshape(tok_rows, heads_here, HEAD_DIM)
    mean_square = jnp.mean(attended * attended, axis=-1, keepdims=True)
    normed = attended * lax.rsqrt(mean_square + 1e-06) * norm_gain.reshape(heads_here, HEAD_DIM)
    normed = normed * jax.nn.silu(gates).reshape(tok_rows, heads_here, HEAD_DIM)
    gated = normed.reshape(tok_rows, heads_here * HEAD_DIM).astype(jnp.bfloat16)
    partial_value = jnp.dot(gated, w_out, preferred_element_type=jnp.float32)
    summed = lax.psum_scatter(
        partial_value.astype(jnp.bfloat16), "head", scatter_dimension=1, tiled=True
    )
    return summed


F32 = jnp.float32
BF16 = jnp.bfloat16
MESH = pl.DeviceIdType.MESH
N_COPIES = 29


def fused_kernel(
    n_tm, frames_hbm, conv, wq, wk, wv, wg, wo, gain, out_hbm,
    frames, own, wo_own, out,
    smooth, qs, ks, vs, gs, wx, wox, gainx, halo, ext_a, ext_b, state, carried,
    total, pair, before, incoming,
    s_tot, r_tot, s_pair, r_pair, s_grp, r_grp, s_bef, r_bef, s_inc, r_inc,
    send_sem, recv_sem, load_sem, store_sem,
):
    t = lax.axis_index("tm")
    h = lax.axis_index("head")
    rows = frames.shape[0]
    half = wq.shape[1]
    heads = half // HEAD_DIM
    blocks = rows // BLOCK
    depth = wq.shape[0]
    quarter = depth // 4
    quarter_o = half // 4
    n_z = n_tm // 4
    z = lax.div(t, 4)
    r = lax.rem(t, 4)
    x = lax.div(r, 2)
    c = lax.rem(t, 2)
    other_core = {"tm": t + 1 - 2 * c}
    other_x = {"tm": t + 2 - 4 * x}
    other_y = {"head": 1 - h}
    after = {"tm": lax.rem(t + 1, n_tm)}
    ahead = {"tm": lax.rem(t + n_tm - 1, n_tm)}
    zs = [{"tm": lax.rem(z + d, n_z) * 4 + r} for d in range(1, n_z)]
    r_x = r + 2 - 4 * x

    loads = {}

    def load(name, src, dst):
        n = len(loads)
        loads[name] = pltpu.make_async_copy(src, dst, load_sem.at[n])
        loads[name].start()

    for b in range(blocks):
        at = pl.ds(b * BLOCK, BLOCK)
        load(b, frames_hbm.at[at, :], frames.at[at, :])
    for m, weight in enumerate((wk, wv, wq, wg)):
        load(("own", m), weight, own.at[m])
    load("out", wo.at[:, pl.ds(pl.multiple_of(h * half, half), half)], wo_own)

    barrier = pltpu.get_barrier_semaphore()
    peers = [other_core, other_x, other_y, after, ahead] + zs
    for peer in peers:
        pl.semaphore_signal(barrier, inc=1, device_id=peer, device_id_type=MESH)
    pl.semaphore_wait(barrier, len(peers))

    copies = []

    def send(src, dst, device):
        n = len(copies)
        copy = pltpu.make_async_remote_copy(
            src_ref=src, dst_ref=dst, send_sem=send_sem.at[n], recv_sem=recv_sem.at[n],
            device_id=device, device_id_type=MESH,
        )
        copy.start()
        copies.append(copy)
        return copy

    def piece(m, which):
        if m == 4:
            return wox.at[pl.ds(pl.multiple_of(which * quarter_o, quarter_o), quarter_o), :]
        return wx.at[m, pl.ds(pl.multiple_of(which * quarter, quarter), quarter), :]

    edge = send(frames_hbm.at[pl.ds(rows - 16, 16), :], halo, after)
    from_y, from_x, from_core = {}, {}, {}

    def start_y(m):
        if m < 4:
            weight = (wk, wv, wq, wg)[m]
            mine = weight.at[pl.ds(pl.multiple_of(r * quarter, quarter), quarter), :]
        else:
            mine = wo.at[
                pl.ds(pl.multiple_of(r * quarter_o, quarter_o), quarter_o),
                pl.ds(pl.multiple_of((1 - h) * half, half), half),
            ]
        from_y[m] = send(mine, piece(m, r), other_y)

    start_y(0)
    gain_copy = send(gain, gainx, other_y)

    def relay_y(m):
        from_y[m].wait_recv()
        from_x[m] = send(piece(m, r), piece(m, r), other_x)
        from_core[m] = [send(piece(m, r), piece(m, r), other_core)]

    def relay_x(m):
        from_x[m].wait_recv()
        from_core[m].append(send(piece(m, r_x), piece(m, r_x), other_core))

    def ready(m):
        for copy in from_core[m]:
            copy.wait_recv()

    chunk = BLOCK // 2
    taps = conv[...].astype(F32)

    def mix(b):
        for part, ext in ((0, ext_a), (1, ext_b)):
            first = b * BLOCK + part * chunk
            if first == 0:
                ext[0:16, :] = halo[...].astype(F32) * jnp.minimum(t, 1).astype(F32)
            else:
                ext[0:16, :] = frames[first - 16 : first, :].astype(F32)
            ext[16 : 16 + chunk, :] = frames[first : first + chunk, :].astype(F32)
            mixed = taps[0:1] * ext[13 : 13 + chunk, :]
            for j in range(1, CONV):
                mixed = mixed + taps[j : j + 1] * ext[13 + j : 13 + j + chunk, :]
            smooth[first : first + chunk, :] = mixed.astype(BF16)

    wide = 2 * HEAD_DIM

    def project_block(at, jobs):
        for weight, into, which, function in jobs:
            for first in range(0, half, wide):
                cols = slice(first, first + wide)
                product = jnp.dot(smooth[at, :], weight[:, cols], preferred_element_type=F32)
                into[which, at, cols] = function(product, cols).astype(BF16)

    def project(jobs):
        def step(i, _):
            for u in range(2):
                project_block(pl.ds(pl.multiple_of((2 * i + u) * BLOCK, BLOCK), BLOCK), jobs)
            return 0

        lax.fori_loop(0, blocks // 2, step, 0)

    def features(v, cols):
        return feature_map(v)

    def silu_by(gain_ref):
        def function(v, cols):
            return (0.5 * v) * (1.0 + jnp.tanh(0.5 * v)) * gain_ref[:, cols]

        return function

    def same(v, cols):
        return v

    def states(which):
        def step(b, _):
            at = pl.ds(pl.multiple_of(b * BLOCK, BLOCK), BLOCK)
            for first in range(0, half, wide):
                cols = slice(first, first + wide)
                both = lax.dot_general(
                    ks[which, at, cols], vs[which, at, cols],
                    (((0,), (0,)), ((), ())), preferred_element_type=F32,
                )
                for j in range(0, wide, HEAD_DIM):
                    state[which, b, first + j : first + j + HEAD_DIM, :] = both[
                        j : j + HEAD_DIM, j : j + HEAD_DIM
                    ]
            return 0

        lax.fori_loop(0, blocks, step, 0)

    def carry(which, start_ref):
        running = start_ref[...].astype(F32)
        for b in range(blocks):
            carried[which, b] = running.astype(BF16)
            if b + 1 < blocks:
                running = running + state[which, b]

    row_id = lax.broadcasted_iota(jnp.int32, (chunk, chunk), 0)
    col_id = lax.broadcasted_iota(jnp.int32, (chunk, chunk), 1)
    causal = col_id <= row_id
    nt = (((1,), (1,)), ((), ()))

    def attend(which, lower, upper):
        def step(b, _):
            low = pl.ds(pl.multiple_of(b * BLOCK, BLOCK), chunk)
            high = pl.ds(pl.multiple_of(b * BLOCK + chunk, chunk), chunk)
            for j in range(heads):
                cols = slice(j * HEAD_DIM, (j + 1) * HEAD_DIM)
                q0, q1 = qs[which, low, cols], qs[which, high, cols]
                k0, k1 = ks[which, low, cols], ks[which, high, cols]
                v0, v1 = vs[which, low, cols], vs[which, high, cols]
                start = carried[which, b, cols, :]
                s00 = lax.dot_general(q0, k0, nt, preferred_element_type=F32)
                s10 = lax.dot_general(q1, k0, nt, preferred_element_type=F32)
                s11 = lax.dot_general(q1, k1, nt, preferred_element_type=F32)
                s00 = jnp.where(causal, s00, 0.0).astype(BF16)
                s11 = jnp.where(causal, s11, 0.0).astype(BF16)
                a0 = jnp.dot(
                    jnp.concatenate([s00, q0], axis=1),
                    jnp.concatenate([v0, start], axis=0), preferred_element_type=F32,
                )
                a1 = jnp.dot(
                    jnp.concatenate([s10.astype(BF16), s11, q1], axis=1),
                    jnp.concatenate([v0, v1, start], axis=0), preferred_element_type=F32,
                )
                for at, a in ((low, a0), (high, a1)):
                    scale = lax.rsqrt(jnp.mean(a * a, axis=-1, keepdims=True) + 1e-06)
                    gated = a * scale * gs[which, at, cols].astype(F32)
                    qs[which, at, cols] = gated.astype(BF16)
            return 0

        lax.fori_loop(lower, upper, step, 0)

    here = pl.ds(pl.multiple_of(c * (half // 2), half // 2), half // 2)
    there = pl.ds(pl.multiple_of((1 - c) * (half // 2), half // 2), half // 2)

    own_kv = [(own.at[0], ks, 0, features), (own.at[1], vs, 0, same)]

    def first_block(b):
        project_block(pl.ds(b * BLOCK, BLOCK), own_kv)

    loads[0].wait()
    for b in range(1, blocks):
        loads[b].wait()
        if b == 2:
            loads["own", 0].wait()
            loads["own", 1].wait()
        mix(b)
        if b > 1:
            first_block(b - 1)
        if b in (1, 3):
            start_y((b + 1) // 2)
    edge.wait_recv()
    mix(0)
    first_block(blocks - 1)
    first_block(0)
    relay_y(0)
    states(0)
    sums = state[0, 0]
    for b in range(1, blocks):
        sums = sums + state[0, b]
    total[...] = sums
    s_tot[...] = sums.astype(BF16)
    tot_copy = send(s_tot, r_tot, other_core)
    loads["own", 2].wait()
    project([(own.at[2], qs, 0, features)])
    start_y(3)
    tot_copy.wait_recv()
    pair[...] = total[...] + r_tot[...].astype(F32)
    s_pair[...] = pair[here, :].astype(BF16)
    pair_copy = send(s_pair, r_pair, other_x)
    relay_y(1)
    loads["own", 3].wait()
    project([(own.at[3], gs, 0, silu_by(gain))])
    start_y(4)
    pair_copy.wait_recv()
    s_grp[...] = (pair[here, :] + r_pair[...].astype(F32)).astype(BF16)
    grp_copies = [send(s_grp, r_grp.at[d], device) for d, device in enumerate(zs)]
    relay_x(0)
    ready(0)
    project([(wx.at[0], ks, 1, features)])
    for copy in grp_copies:
        copy.wait_recv()
    sums = r_pair[...].astype(F32) * x.astype(F32)
    for d in range(1, n_z):
        earlier = jnp.where(z >= d, 1.0, 0.0)
        sums = sums + r_grp[d - 1].astype(F32) * earlier
    before[...] = sums
    s_bef[...] = sums.astype(BF16)
    bef_copy = send(s_bef, r_bef, other_core)
    relay_y(2)
    relay_x(1)
    ready(1)
    project([(wx.at[1], vs, 1, same)])
    states(1)
    bef_copy.wait_recv()
    incoming[here, :] = before[...]
    incoming[there, :] = r_bef[...].astype(F32)
    incoming[...] = incoming[...] + r_tot[...].astype(F32) * c.astype(F32)
    s_inc[...] = incoming[...].astype(BF16)
    inc_copy = send(s_inc, r_inc, other_y)
    carry(0, incoming)
    attend(0, 0, blocks // 2)
    relay_y(3)
    relay_x(2)
    attend(0, blocks // 2, blocks)
    relay_y(4)
    ready(2)
    project([(wx.at[2], qs, 1, features)])
    relay_x(3)
    ready(3)
    gain_copy.wait_recv()
    project([(wx.at[3], gs, 1, silu_by(gainx))])
    relay_x(4)
    inc_copy.wait_recv()
    carry(1, r_inc)
    attend(1, 0, blocks)
    ready(4)

    loads["out"].wait()
    stores = []
    for b in range(blocks):
        at = pl.ds(b * BLOCK, BLOCK)
        for first in range(0, half, wide):
            cols = slice(first, first + wide)
            here_part = jnp.dot(qs[0, at, :], wo_own[:, cols], preferred_element_type=F32)
            there_part = jnp.dot(qs[1, at, :], wox[:, cols], preferred_element_type=F32)
            out[at, cols] = (here_part + there_part).astype(BF16)
        store = pltpu.make_async_copy(out.at[at, :], out_hbm.at[at, :], store_sem.at[b])
        store.start()
        stores.append(store)
    for store in stores:
        store.wait()
    for copy in copies:
        copy.wait_send()


def on_device_fused(n_tm, frames, conv_weight, w_query, w_key, w_value, w_gate, w_out, norm_gain):
    rows, depth = frames.shape
    half = w_query.shape[1]
    blocks = rows // BLOCK
    chunk = BLOCK // 2
    state_rows = half
    vmem = pl.BlockSpec(memory_space=pltpu.VMEM)
    hbm = pl.BlockSpec(memory_space=pl.ANY)
    act = pltpu.VMEM((2, rows, half), BF16)
    whole = (state_rows, HEAD_DIM)
    split = (state_rows // 2, HEAD_DIM)
    return pl.pallas_call(
        functools.partial(fused_kernel, n_tm),
        out_shape=jax.ShapeDtypeStruct((rows, half), BF16),
        in_specs=[hbm, vmem] + [hbm] * 5 + [vmem],
        out_specs=hbm,
        scratch_shapes=[
            pltpu.VMEM((rows, depth), BF16),
            pltpu.VMEM((4, depth, half), BF16),
            pltpu.VMEM((half, half), BF16),
            pltpu.VMEM((rows, half), BF16),
            pltpu.VMEM((rows, depth), BF16),
            act, act, act, act,
            pltpu.VMEM((4, depth, half), BF16),
            pltpu.VMEM((half, half), BF16),
            pltpu.VMEM((1, half), F32),
            pltpu.VMEM((16, depth), BF16),
            pltpu.VMEM((16 + chunk, depth), F32),
            pltpu.VMEM((16 + chunk, depth), F32),
            pltpu.VMEM((2, blocks) + whole, F32),
            pltpu.VMEM((2, blocks) + whole, BF16),
            pltpu.VMEM(whole, F32),
            pltpu.VMEM(whole, F32),
            pltpu.VMEM(split, F32),
            pltpu.VMEM(whole, F32),
            pltpu.VMEM(whole, BF16), pltpu.VMEM(whole, BF16),
            pltpu.VMEM(split, BF16), pltpu.VMEM(split, BF16),
            pltpu.VMEM(split, BF16), pltpu.VMEM((n_tm // 4 - 1,) + split, BF16),
            pltpu.VMEM(split, BF16), pltpu.VMEM(split, BF16),
            pltpu.VMEM(whole, BF16), pltpu.VMEM(whole, BF16),
            pltpu.SemaphoreType.DMA((N_COPIES,)),
            pltpu.SemaphoreType.DMA((N_COPIES,)),
            pltpu.SemaphoreType.DMA((blocks + 5,)),
            pltpu.SemaphoreType.DMA((blocks,)),
        ],
        compiler_params=pltpu.CompilerParams(
            collective_id=0, has_side_effects=True, vmem_limit_bytes=60 * 2**20
        ),
    )(frames, conv_weight, w_query, w_key, w_value, w_gate, w_out, norm_gain.reshape(1, half))


def solution(mesh):
    placed = (
        P("tm", None),
        P(),
        P(None, "head"),
        P(None, "head"),
        P(None, "head"),
        P(None, "head"),
        P("head", None),
        P("head"),
    )
    n_tm = mesh.shape["tm"]
    if mesh.shape["head"] == 2 and n_tm == 16:
        on_device = functools.partial(on_device_fused, n_tm)
    else:
        on_device = on_device_collectives
    return jax.shard_map(
        on_device, mesh=mesh, in_specs=placed, out_specs=P("tm", "head"), check_vma=False
    )
```

```python
import functools

import jax
import jax.numpy as jnp
from jax import lax
from jax.experimental import pallas as pl
from jax.experimental.pallas import tpu as pltpu
from jax.sharding import PartitionSpec as P

HEAD_DIM = 128
CONV = 4
BLOCK = 512


def from_behind(array, axis, by):
    devices = lax.axis_size(axis)
    pairs = [(i, i + by) for i in range(devices) if 0 <= i + by < devices]
    return lax.ppermute(array, axis, pairs)


def feature_map(inputs):
    return jnp.where(inputs > 0, inputs + 1.0, jnp.exp(jnp.minimum(inputs, 0.0)))


def on_device_collectives(frames, conv_weight, w_query, w_key, w_value, w_gate, w_out, norm_gain):
    tok_rows = frames.shape[0]
    edge_rows = from_behind(frames[tok_rows - (CONV - 1) :], "tm", 1)
    padded = jnp.concatenate([edge_rows, frames], axis=0)
    taps = conv_weight.astype(jnp.float32)
    mixed = taps[0] * padded[0:tok_rows].astype(jnp.float32)
    for offset in range(1, CONV):
        mixed = mixed + taps[offset] * padded[offset : offset + tok_rows].astype(jnp.float32)
    smooth = mixed.astype(jnp.bfloat16)
    queries = feature_map(jnp.dot(smooth, w_query, preferred_element_type=jnp.float32)).astype(
        jnp.bfloat16
    )
    key_feats = feature_map(jnp.dot(smooth, w_key, preferred_element_type=jnp.float32)).astype(
        jnp.bfloat16
    )
    values = jnp.dot(smooth, w_value, preferred_element_type=jnp.float32).astype(jnp.bfloat16)
    gates = jnp.dot(smooth, w_gate, preferred_element_type=jnp.float32)
    heads_here = w_query.shape[1] // HEAD_DIM
    blocks = tok_rows // BLOCK
    block_shape = (blocks, BLOCK, heads_here, HEAD_DIM)
    query_blocks = queries.reshape(block_shape)
    key_blocks = key_feats.reshape(block_shape)
    value_blocks = values.reshape(block_shape)
    block_states = jnp.einsum(
        "bthd,bthe->bhde", key_blocks, value_blocks, preferred_element_type=jnp.float32
    )
    own_total = jnp.sum(block_states, axis=0)
    position = lax.axis_index("tm")
    shard_piece = lax.all_gather(own_total[None], "tm", axis=0, tiled=True)
    source_rank = jnp.arange(shard_piece.shape[0], dtype=jnp.int32)
    earlier_mask = (source_rank < position).astype(jnp.float32)
    incoming = jnp.sum(shard_piece * earlier_mask[:, None, None, None], axis=0)
    running_sums = jnp.cumsum(block_states, axis=0)
    exclusive = jnp.concatenate([jnp.zeros_like(block_states[:1]), running_sums[:-1]], axis=0)
    carried = (incoming[None] + exclusive).astype(jnp.bfloat16)
    causal = jnp.tril(jnp.ones((BLOCK, BLOCK), jnp.bool_))
    scores = jnp.einsum(
        "bthd,bshd->bhts", query_blocks, key_blocks, preferred_element_type=jnp.float32
    )
    scores = jnp.where(causal[None, None], scores, 0.0).astype(jnp.bfloat16)
    attended = jnp.einsum(
        "bhts,bshd->bthd", scores, value_blocks, preferred_element_type=jnp.float32
    )
    attended = attended + jnp.einsum(
        "bthd,bhde->bthe", query_blocks, carried, preferred_element_type=jnp.float32
    )
    attended = attended.reshape(tok_rows, heads_here, HEAD_DIM)
    mean_square = jnp.mean(attended * attended, axis=-1, keepdims=True)
    normed = attended * lax.rsqrt(mean_square + 1e-06) * norm_gain.reshape(heads_here, HEAD_DIM)
    normed = normed * jax.nn.silu(gates).reshape(tok_rows, heads_here, HEAD_DIM)
    gated = normed.reshape(tok_rows, heads_here * HEAD_DIM).astype(jnp.bfloat16)
    partial_value = jnp.dot(gated, w_out, preferred_element_type=jnp.float32)
    summed = lax.psum_scatter(
        partial_value.astype(jnp.bfloat16), "head", scatter_dimension=1, tiled=True
    )
    return summed


F32 = jnp.float32
BF16 = jnp.bfloat16
MESH = pl.DeviceIdType.MESH
N_COPIES = 29


def fused_kernel(
    n_tm, frames_hbm, conv, wq, wk, wv, wg, wo, gain, out_hbm,
    frames, own, wo_own, out,
    smooth, qs, ks, vs, gs, wx, wox, gainx, halo, ext_a, ext_b, state, carried,
    total, pair, before, incoming,
    s_tot, r_tot, s_pair, r_pair, s_grp, r_grp, s_bef, r_bef, s_inc, r_inc,
    send_sem, recv_sem, load_sem, store_sem,
):
    t = lax.axis_index("tm")
    h = lax.axis_index("head")
    rows = frames.shape[0]
    half = wq.shape[1]
    heads = half // HEAD_DIM
    blocks = rows // BLOCK
    depth = wq.shape[0]
    quarter = depth // 4
    quarter_o = half // 4
    n_z = n_tm // 4
    z = lax.div(t, 4)
    r = lax.rem(t, 4)
    x = lax.div(r, 2)
    c = lax.rem(t, 2)
    other_core = {"tm": t + 1 - 2 * c}
    other_x = {"tm": t + 2 - 4 * x}
    other_y = {"head": 1 - h}
    after = {"tm": lax.rem(t + 1, n_tm)}
    ahead = {"tm": lax.rem(t + n_tm - 1, n_tm)}
    zs = [{"tm": lax.rem(z + d, n_z) * 4 + r} for d in range(1, n_z)]
    r_x = r + 2 - 4 * x

    loads = {}

    def load(name, src, dst):
        n = len(loads)
        loads[name] = pltpu.make_async_copy(src, dst, load_sem.at[n])
        loads[name].start()

    for b in range(blocks):
        at = pl.ds(b * BLOCK, BLOCK)
        load(b, frames_hbm.at[at, :], frames.at[at, :])
    for m, weight in enumerate((wk, wv, wq, wg)):
        load(("own", m), weight, own.at[m])
    load("out", wo.at[:, pl.ds(pl.multiple_of(h * half, half), half)], wo_own)

    barrier = pltpu.get_barrier_semaphore()
    peers = [other_core, other_x, other_y, after, ahead] + zs
    for peer in peers:
        pl.semaphore_signal(barrier, inc=1, device_id=peer, device_id_type=MESH)
    pl.semaphore_wait(barrier, len(peers))

    copies = []

    def send(src, dst, device):
        n = len(copies)
        copy = pltpu.make_async_remote_copy(
            src_ref=src, dst_ref=dst, send_sem=send_sem.at[n], recv_sem=recv_sem.at[n],
            device_id=device, device_id_type=MESH,
        )
        copy.start()
        copies.append(copy)
        return copy

    def piece(m, which):
        if m == 4:
            return wox.at[pl.ds(pl.multiple_of(which * quarter_o, quarter_o), quarter_o), :]
        return wx.at[m, pl.ds(pl.multiple_of(which * quarter, quarter), quarter), :]

    edge = send(frames_hbm.at[pl.ds(rows - 16, 16), :], halo, after)
    from_y, from_x, from_core = {}, {}, {}

    def start_y(m):
        if m < 4:
            weight = (wk, wv, wq, wg)[m]
            mine = weight.at[pl.ds(pl.multiple_of(r * quarter, quarter), quarter), :]
        else:
            mine = wo.at[
                pl.ds(pl.multiple_of(r * quarter_o, quarter_o), quarter_o),
                pl.ds(pl.multiple_of((1 - h) * half, half), half),
            ]
        from_y[m] = send(mine, piece(m, r), other_y)

    start_y(0)
    gain_copy = send(gain, gainx, other_y)

    def relay_y(m):
        from_y[m].wait_recv()
        from_x[m] = send(piece(m, r), piece(m, r), other_x)
        from_core[m] = [send(piece(m, r), piece(m, r), other_core)]

    def relay_x(m):
        from_x[m].wait_recv()
        from_core[m].append(send(piece(m, r_x), piece(m, r_x), other_core))

    def ready(m):
        for copy in from_core[m]:
            copy.wait_recv()

    chunk = BLOCK // 2
    taps = conv[...].astype(F32)

    def mix(b):
        for part, ext in ((0, ext_a), (1, ext_b)):
            first = b * BLOCK + part * chunk
            if first == 0:
                ext[0:16, :] = halo[...].astype(F32) * jnp.minimum(t, 1).astype(F32)
            else:
                ext[0:16, :] = frames[first - 16 : first, :].astype(F32)
            ext[16 : 16 + chunk, :] = frames[first : first + chunk, :].astype(F32)
            mixed = taps[0:1] * ext[13 : 13 + chunk, :]
            for j in range(1, CONV):
                mixed = mixed + taps[j : j + 1] * ext[13 + j : 13 + j + chunk, :]
            smooth[first : first + chunk, :] = mixed.astype(BF16)

    wide = 2 * HEAD_DIM

    def project_block(at, jobs):
        for weight, into, which, function in jobs:
            for first in range(0, half, wide):
                cols = slice(first, first + wide)
                product = jnp.dot(smooth[at, :], weight[:, cols], preferred_element_type=F32)
                into[which, at, cols] = function(product, cols).astype(BF16)

    def project(jobs):
        for b in range(blocks):
            project_block(pl.ds(b * BLOCK, BLOCK), jobs)

    def features(v, cols):
        return feature_map(v)

    def silu_by(gain_ref):
        def function(v, cols):
            return (0.5 * v) * (1.0 + jnp.tanh(0.5 * v)) * gain_ref[:, cols]

        return function

    def same(v, cols):
        return v

    def states(which):
        def step(b, _):
            at = pl.ds(pl.multiple_of(b * BLOCK, BLOCK), BLOCK)
            for first in range(0, half, wide):
                cols = slice(first, first + wide)
                both = lax.dot_general(
                    ks[which, at, cols], vs[which, at, cols],
                    (((0,), (0,)), ((), ())), preferred_element_type=F32,
                )
                for j in range(0, wide, HEAD_DIM):
                    state[which, b, first + j : first + j + HEAD_DIM, :] = both[
                        j : j + HEAD_DIM, j : j + HEAD_DIM
                    ]
            return 0

        lax.fori_loop(0, blocks, step, 0)

    def carry(which, start_ref):
        running = start_ref[...].astype(F32)
        for b in range(blocks):
            carried[which, b] = running.astype(BF16)
            if b + 1 < blocks:
                running = running + state[which, b]

    row_id = lax.broadcasted_iota(jnp.int32, (chunk, chunk), 0)
    col_id = lax.broadcasted_iota(jnp.int32, (chunk, chunk), 1)
    causal = col_id <= row_id
    nt = (((1,), (1,)), ((), ()))

    def attend(which, lower, upper):
        def one(b):
            low = pl.ds(pl.multiple_of(b * BLOCK, BLOCK), chunk)
            high = pl.ds(pl.multiple_of(b * BLOCK + chunk, chunk), chunk)
            for j in range(heads):
                cols = slice(j * HEAD_DIM, (j + 1) * HEAD_DIM)
                q0, q1 = qs[which, low, cols], qs[which, high, cols]
                k0, k1 = ks[which, low, cols], ks[which, high, cols]
                v0, v1 = vs[which, low, cols], vs[which, high, cols]
                start = carried[which, b, cols, :]
                s00 = lax.dot_general(q0, k0, nt, preferred_element_type=F32)
                s10 = lax.dot_general(q1, k0, nt, preferred_element_type=F32)
                s11 = lax.dot_general(q1, k1, nt, preferred_element_type=F32)
                s00 = jnp.where(causal, s00, 0.0).astype(BF16)
                s11 = jnp.where(causal, s11, 0.0).astype(BF16)
                a0 = jnp.dot(
                    jnp.concatenate([s00, q0], axis=1),
                    jnp.concatenate([v0, start], axis=0), preferred_element_type=F32,
                )
                a1 = jnp.dot(
                    jnp.concatenate([s10.astype(BF16), s11, q1], axis=1),
                    jnp.concatenate([v0, v1, start], axis=0), preferred_element_type=F32,
                )
                for at, a in ((low, a0), (high, a1)):
                    scale = lax.rsqrt(jnp.mean(a * a, axis=-1, keepdims=True) + 1e-06)
                    gated = a * scale * gs[which, at, cols].astype(F32)
                    qs[which, at, cols] = gated.astype(BF16)
        def step(i, _):
            one(2 * i)
            one(2 * i + 1)
            return 0

        lax.fori_loop(lower // 2, upper // 2, step, 0)

    here = pl.ds(pl.multiple_of(c * (half // 2), half // 2), half // 2)
    there = pl.ds(pl.multiple_of((1 - c) * (half // 2), half // 2), half // 2)

    own_kv = [(own.at[0], ks, 0, features), (own.at[1], vs, 0, same)]

    def first_block(b):
        project_block(pl.ds(b * BLOCK, BLOCK), own_kv)

    loads[0].wait()
    for b in range(1, blocks):
        loads[b].wait()
        if b == 2:
            loads["own", 0].wait()
            loads["own", 1].wait()
        mix(b)
        if b > 1:
            first_block(b - 1)
        if b in (1, 3):
            start_y((b + 1) // 2)
    edge.wait_recv()
    mix(0)
    first_block(blocks - 1)
    first_block(0)
    relay_y(0)
    states(0)
    sums = state[0, 0]
    for b in range(1, blocks):
        sums = sums + state[0, b]
    total[...] = sums
    s_tot[...] = sums.astype(BF16)
    tot_copy = send(s_tot, r_tot, other_core)
    loads["own", 2].wait()
    project([(own.at[2], qs, 0, features)])
    start_y(3)
    tot_copy.wait_recv()
    pair[...] = total[...] + r_tot[...].astype(F32)
    s_pair[...] = pair[here, :].astype(BF16)
    pair_copy = send(s_pair, r_pair, other_x)
    relay_y(1)
    loads["own", 3].wait()
    project([(own.at[3], gs, 0, silu_by(gain))])
    start_y(4)
    pair_copy.wait_recv()
    s_grp[...] = (pair[here, :] + r_pair[...].astype(F32)).astype(BF16)
    grp_copies = [send(s_grp, r_grp.at[d], device) for d, device in enumerate(zs)]
    relay_x(0)
    ready(0)
    project([(wx.at[0], ks, 1, features)])
    for copy in grp_copies:
        copy.wait_recv()
    sums = r_pair[...].astype(F32) * x.astype(F32)
    for d in range(1, n_z):
        earlier = jnp.where(z >= d, 1.0, 0.0)
        sums = sums + r_grp[d - 1].astype(F32) * earlier
    before[...] = sums
    s_bef[...] = sums.astype(BF16)
    bef_copy = send(s_bef, r_bef, other_core)
    relay_y(2)
    relay_x(1)
    ready(1)
    project([(wx.at[1], vs, 1, same)])
    states(1)
    bef_copy.wait_recv()
    incoming[here, :] = before[...]
    incoming[there, :] = r_bef[...].astype(F32)
    incoming[...] = incoming[...] + r_tot[...].astype(F32) * c.astype(F32)
    s_inc[...] = incoming[...].astype(BF16)
    inc_copy = send(s_inc, r_inc, other_y)
    carry(0, incoming)
    attend(0, 0, blocks // 2)
    relay_y(3)
    relay_x(2)
    attend(0, blocks // 2, blocks)
    relay_y(4)
    ready(2)
    project([(wx.at[2], qs, 1, features)])
    relay_x(3)
    ready(3)
    gain_copy.wait_recv()
    project([(wx.at[3], gs, 1, silu_by(gainx))])
    relay_x(4)
    inc_copy.wait_recv()
    carry(1, r_inc)
    attend(1, 0, blocks)
    ready(4)

    loads["out"].wait()
    stores = []
    for b in range(blocks):
        at = pl.ds(b * BLOCK, BLOCK)
        for first in range(0, half, wide):
            cols = slice(first, first + wide)
            here_part = jnp.dot(qs[0, at, :], wo_own[:, cols], preferred_element_type=F32)
            there_part = jnp.dot(qs[1, at, :], wox[:, cols], preferred_element_type=F32)
            out[at, cols] = (here_part + there_part).astype(BF16)
        store = pltpu.make_async_copy(out.at[at, :], out_hbm.at[at, :], store_sem.at[b])
        store.start()
        stores.append(store)
    for store in stores:
        store.wait()
    for copy in copies:
        copy.wait_send()


def on_device_fused(n_tm, frames, conv_weight, w_query, w_key, w_value, w_gate, w_out, norm_gain):
    rows, depth = frames.shape
    half = w_query.shape[1]
    blocks = rows // BLOCK
    chunk = BLOCK // 2
    state_rows = half
    vmem = pl.BlockSpec(memory_space=pltpu.VMEM)
    hbm = pl.BlockSpec(memory_space=pl.ANY)
    act = pltpu.VMEM((2, rows, half), BF16)
    whole = (state_rows, HEAD_DIM)
    split = (state_rows // 2, HEAD_DIM)
    return pl.pallas_call(
        functools.partial(fused_kernel, n_tm),
        out_shape=jax.ShapeDtypeStruct((rows, half), BF16),
        in_specs=[hbm, vmem] + [hbm] * 5 + [vmem],
        out_specs=hbm,
        scratch_shapes=[
            pltpu.VMEM((rows, depth), BF16),
            pltpu.VMEM((4, depth, half), BF16),
            pltpu.VMEM((half, half), BF16),
            pltpu.VMEM((rows, half), BF16),
            pltpu.VMEM((rows, depth), BF16),
            act, act, act, act,
            pltpu.VMEM((4, depth, half), BF16),
            pltpu.VMEM((half, half), BF16),
            pltpu.VMEM((1, half), F32),
            pltpu.VMEM((16, depth), BF16),
            pltpu.VMEM((16 + chunk, depth), F32),
            pltpu.VMEM((16 + chunk, depth), F32),
            pltpu.VMEM((2, blocks) + whole, F32),
            pltpu.VMEM((2, blocks) + whole, BF16),
            pltpu.VMEM(whole, F32),
            pltpu.VMEM(whole, F32),
            pltpu.VMEM(split, F32),
            pltpu.VMEM(whole, F32),
            pltpu.VMEM(whole, BF16), pltpu.VMEM(whole, BF16),
            pltpu.VMEM(split, BF16), pltpu.VMEM(split, BF16),
            pltpu.VMEM(split, BF16), pltpu.VMEM((n_tm // 4 - 1,) + split, BF16),
            pltpu.VMEM(split, BF16), pltpu.VMEM(split, BF16),
            pltpu.VMEM(whole, BF16), pltpu.VMEM(whole, BF16),
            pltpu.SemaphoreType.DMA((N_COPIES,)),
            pltpu.SemaphoreType.DMA((N_COPIES,)),
            pltpu.SemaphoreType.DMA((blocks + 5,)),
            pltpu.SemaphoreType.DMA((blocks,)),
        ],
        compiler_params=pltpu.CompilerParams(
            collective_id=0, has_side_effects=True, vmem_limit_bytes=60 * 2**20
        ),
    )(frames, conv_weight, w_query, w_key, w_value, w_gate, w_out, norm_gain.reshape(1, half))


def solution(mesh):
    placed = (
        P("tm", None),
        P(),
        P(None, "head"),
        P(None, "head"),
        P(None, "head"),
        P(None, "head"),
        P("head", None),
        P("head"),
    )
    n_tm = mesh.shape["tm"]
    if mesh.shape["head"] == 2 and n_tm == 16:
        on_device = functools.partial(on_device_fused, n_tm)
    else:
        on_device = on_device_collectives
    return jax.shard_map(
        on_device, mesh=mesh, in_specs=placed, out_specs=P("tm", "head"), check_vma=False
    )
```
